512 devices in a mesh: lat: 16 (over z, core), tgt: 16 (over x_lo, y), tok: 2 (over x_hi).
Axes of the slice: x: 4 (x_hi: 2, x_lo: 2; x = x_hi * 2 + x_lo), y: 8, z: 8, core: 2. Of those that a mesh axis runs over, the one named last changes fastest.
Arguments:
- errors: bfloat16 [16, 2048, 4096], P('tgt', 'tok', 'lat'), may hold values from -6 to 6
- decoder: bfloat16 [16, 4096, 4096], P('tgt', 'lat'), may hold values from -0.0234375 to 0.0234375
- pre_acts: bfloat16 [2048, 4096], P('tok', 'lat'), may hold values from -0.796875 to 0.796875
- inputs: bfloat16 [2048, 4096], P('tok', 'tgt'), may hold values from -0.796875 to 0.796875
- encoder: bfloat16 [4096, 4096], P('tgt', 'lat'), may hold values from -0.1875 to 0.1875
- block_mask: int32 [16, 32], P('tok', 'lat'), may hold values from 0 to 1, as said below
Outputs:
- dec_grad: bfloat16 [16, 4096, 4096], P('tgt', 'lat', 'tok')
- enc_grad: float32 [4096, 4096], P(('tgt', 'tok'), 'lat')
- input_grad: bfloat16 [2048, 4096], P('tok', 'tgt')
The draws below stay inside these ranges and needn't reach their ends.
Inputs may be any that keep to these rules, and one draw needn't show every extreme that they name: `block_mask`: 1 marks an active block of 128 tokens by 128 latents, 0 an inactive one.
All inputs are finite; a program needn't handle non-finite values.
Results may differ from the reference program's by a relative error of at most 0.0051.
Values may be sent and summed in bfloat16 or wider, within the bound.
No kernel may reach another device: no remote copies, remote signals or barrier semaphores. Data moves between devices by JAX's collectives and lax.ppermute only.
A program may use at most 64 MiB of HBM per device.

```python
import jax
import jax.numpy as jnp
from jax import lax

D = 4096
BLOCK = 128
TOK_DEV = 1024
LATENTS = 4096
LAYERS = 16
TOKENS = 2048
TOK_BLOCKS = 16
LAT_BLOCKS = 32
N_TOK = 2


def draw_block_mask(key, part):
    key = jax.random.fold_in(key, 7)
    level_key, cell_key = jax.random.split(key)
    powers = jax.random.randint(level_key, (1, LAT_BLOCKS), 0, 4)
    levels = jnp.left_shift(jnp.ones_like(powers), powers)
    cells = jax.random.randint(cell_key, (TOK_BLOCKS, LAT_BLOCKS), 0, 8)
    mask = (cells < levels).astype(jnp.int32)
    return mask.at[0, 0].set(1).at[0, 1].set(0)


def shard_levels(stream_key, shape, pieces, smallest, top_value):
    def one(position, blocks):
        heights = jax.random.uniform(jax.random.fold_in(jax.random.fold_in(stream_key, 6), position), (blocks,), jnp.float32, smallest / len(pieces), top_value / len(pieces))
        return jnp.repeat(jnp.exp(heights), shape[position] // blocks).reshape((-1,) + (1,) * (len(shape) - position - 1))

    gain = one(*pieces[0])
    for cut in pieces[1:]:
        gain = gain * one(*cut)
    return gain


def noise(own_key, extent, deviation, most, cuts=(), held_as=jnp.bfloat16):
    loudness = shard_levels(own_key, extent, cuts, -0.22, 0.18) if cuts else 1.0
    values = jax.random.normal(own_key, extent, jnp.float32) * deviation * loudness
    return jnp.minimum(jnp.maximum(values, -most), most).astype(held_as)


def setup_inputs(seed: int = 0) -> dict:
    streams_of = jax.random.split(jax.random.key(seed), 7)
    errors = noise(streams_of[0], (LAYERS, TOKENS, D), 1.0, 6.0, ((0, 16), (1, 2), (2, 16)))
    decoder = noise(streams_of[1], (LAYERS, LATENTS, D), (LAYERS * D) ** -0.5, 0.0234375, ((0, 16), (1, 16)))
    pre_acts = noise(streams_of[2], (TOKENS, LATENTS), 0.1, 0.796875, ((0, 2), (1, 16)))
    inputs = noise(streams_of[3], (TOKENS, D), 0.1, 0.796875, ((0, 2), (1, 16)))
    encoder = noise(streams_of[4], (D, LATENTS), (LATENTS // 4) ** -0.5, 0.1875, ((0, 16), (1, 16)))
    block_mask = draw_block_mask(jax.random.fold_in(streams_of[6], 71), 0)
    return {"errors": errors, "decoder": decoder, "pre_acts": pre_acts, "inputs": inputs, "encoder": encoder, "block_mask": block_mask}


def reference(errors, decoder, pre_acts, inputs, encoder, block_mask):
    cells = jnp.repeat(jnp.repeat(block_mask, BLOCK, axis=0), BLOCK, axis=1)
    live = (cells > 0) & (pre_acts > 0)
    latents = jnp.where(live, pre_acts, jnp.zeros_like(pre_acts))
    halves = latents.reshape(N_TOK, TOK_DEV, LATENTS)

    def layer_step(total, pair):
        layer_err, weights = pair
        grad = jnp.dot(layer_err, weights.T, preferred_element_type=jnp.float32)
        err_halves = layer_err.reshape(N_TOK, TOK_DEV, D)
        summed = jnp.zeros((LATENTS, D), jnp.float32)
        for which in range(N_TOK):
            part = jnp.dot(halves[which].T, err_halves[which], preferred_element_type=jnp.float32)
            summed = summed + lax.optimization_barrier(part.astype(jnp.bfloat16)).astype(jnp.float32)
        return total + grad, summed.astype(jnp.bfloat16)

    start = jnp.zeros((TOKENS, LATENTS), jnp.float32)
    latent_grad, dec_grad = lax.scan(layer_step, start, (errors, decoder))
    delta = jnp.where(live, latent_grad, jnp.zeros_like(latent_grad)).astype(jnp.bfloat16)
    enc_grad = jnp.dot(inputs.T, delta, preferred_element_type=jnp.float32)
    input_grad = jnp.dot(delta, encoder.T, preferred_element_type=jnp.float32).astype(jnp.bfloat16)
    return (dec_grad, enc_grad, input_grad)
```

```python
import functools

import jax
import jax.numpy as jnp
from jax import lax
from jax.experimental import pallas as pl
from jax.experimental.pallas import tpu as pltpu
from jax.sharding import PartitionSpec as P

F32 = jnp.float32
BF16 = jnp.bfloat16


def products_kernel(err_ref, dec_ref, lat_t_ref, live_ref, grad_ref, part_ref, total):
    step = pl.program_id(0)
    err = err_ref[0]
    term = lax.dot_general(err, dec_ref[...], (((1,), (1,)), ((), ())), preferred_element_type=F32)

    @pl.when(step == 0)
    def _():
        total[...] = term

    @pl.when(step > 0)
    def _():
        total[...] += term

    part_ref[...] = jnp.dot(lat_t_ref[...], err, preferred_element_type=F32).astype(BF16)

    @pl.when(step == pl.num_programs(0) - 1)
    def _():
        grad_ref[...] = jnp.where(live_ref[...] > 0, total[...], 0.0).astype(BF16)


def products(whole, weights, lat_t, latents):
    n, tokens, width = whole.shape
    rows = weights.shape[0]
    return pl.pallas_call(
        products_kernel,
        grid=(n,),
        in_specs=[
            pl.BlockSpec((1, tokens, width), lambda i: (i, 0, 0)),
            pl.BlockSpec((rows, width), lambda i: (0, i)),
            pl.BlockSpec((rows, tokens), lambda i: (0, 0)),
            pl.BlockSpec((tokens, rows), lambda i: (0, 0)),
        ],
        out_specs=[
            pl.BlockSpec((tokens, rows), lambda i: (0, 0)),
            pl.BlockSpec((rows, width), lambda i: (0, i)),
        ],
        out_shape=[
            jax.ShapeDtypeStruct((tokens, rows), BF16),
            jax.ShapeDtypeStruct((rows, n * width), BF16),
        ],
        scratch_shapes=[pltpu.VMEM((tokens, rows), F32)],
        compiler_params=pltpu.CompilerParams(vmem_limit_bytes=32 * 1024 * 1024),
        cost_estimate=pl.CostEstimate(
            flops=4 * n * tokens * width * rows,
            bytes_accessed=2 * n * tokens * width + 4 * rows * n * width,
            transcendentals=0,
        ),
    )(whole, weights, lat_t, latents)


def scatter_sum(terms, axis):
    n = lax.axis_size(axis)
    got = lax.all_to_all(terms.reshape(n, terms.shape[0] // n, terms.shape[1]), axis, 0, 0)
    return jnp.sum(got.astype(F32), axis=0)


def gather(chunk, axis):
    n = lax.axis_size(axis)
    got = lax.all_to_all(jnp.broadcast_to(chunk[None], (n,) + chunk.shape), axis, 0, 0)
    return got.reshape(n * chunk.shape[0], chunk.shape[1])


def shards(errors, decoder, pre_acts, inputs, encoder, block_mask):
    block = pre_acts.shape[0] // block_mask.shape[0]
    cells = jnp.repeat(jnp.repeat(block_mask, block, axis=0), block, axis=1)
    live = (cells > 0) & (pre_acts > 0)
    latents = jnp.where(live, pre_acts, jnp.zeros_like(pre_acts))
    whole = lax.all_gather(errors[0], "lat", axis=0, tiled=False)
    grad_part, dec_part = products(whole, decoder[0], latents.T, latents)
    half = dec_part.shape[1] // 2
    mine = lax.axis_index("tok")
    keep = lax.dynamic_slice_in_dim(dec_part, mine * half, half, 1)
    send = lax.dynamic_slice_in_dim(dec_part, (1 - mine) * half, half, 1)
    other = lax.ppermute(send, "tok", [(0, 1), (1, 0)])
    dec_grad = (keep.astype(F32) + other.astype(F32)).astype(BF16)[None]

    delta_chunk = scatter_sum(grad_part, "tgt").astype(BF16)
    delta = gather(delta_chunk, "tgt")
    enc_part = lax.dot_general(inputs, delta, (((0,), (0,)), ((), ())), preferred_element_type=F32)
    rows = enc_part.shape[0] // 2
    enc_keep = lax.dynamic_slice_in_dim(enc_part, mine * rows, rows, 0)
    enc_send = lax.dynamic_slice_in_dim(enc_part, (1 - mine) * rows, rows, 0)
    enc_grad = enc_keep + lax.ppermute(enc_send, "tok", [(0, 1), (1, 0)])

    input_part = lax.dot_general(delta, encoder, (((1,), (1,)), ((), ())), preferred_element_type=F32)
    input_grad = gather(scatter_sum(input_part.astype(BF16), "lat").astype(BF16), "lat")
    return (dec_grad, enc_grad, input_grad)


def solution(mesh):
    in_specs = (
        P("tgt", "tok", "lat"),
        P("tgt", "lat", None),
        P("tok", "lat"),
        P("tok", "tgt"),
        P("tgt", "lat"),
        P("tok", "lat"),
    )
    out_specs = (P("tgt", "lat", "tok"), P(("tgt", "tok"), "lat"), P("tok", "tgt"))
    return jax.shard_map(shards, mesh=mesh, in_specs=in_specs, out_specs=out_specs, check_vma=False)
```

```python
import functools

import jax
import jax.numpy as jnp
from jax import lax
from jax.experimental import pallas as pl
from jax.experimental.pallas import tpu as pltpu
from jax.sharding import PartitionSpec as P

F32 = jnp.float32
BF16 = jnp.bfloat16
VMEM_BYTES = 20 * 1024 * 1024
COST = pl.CostEstimate(flops=1, bytes_accessed=1, transcendentals=0)
SMEM = pl.BlockSpec(memory_space=pltpu.SMEM)
VMEM = pl.BlockSpec(memory_space=pltpu.VMEM)


def nt(a, b):
    return lax.dot_general(a, b, (((1,), (1,)), ((), ())), preferred_element_type=F32)


def chunk_at(here, distance, nz):
    return lax.rem(here[0] + (2 * here[1] - 1) * distance + nz, nz)


def column(chunk, core, width):
    return pl.ds(pl.multiple_of((2 * chunk + core) * width, width), width)


def step_kernel(plan, distance, here, *refs):
    sibling, carried, carried_s, stacked = plan
    refs = list(refs)
    ex, ey, weights, lat_t = (refs.pop(0) for _ in range(4))
    if sibling:
        weights_s, lat_s = refs.pop(0), refs.pop(0)
    total_in = refs.pop(0) if carried else None
    total_s_in = refs.pop(0) if carried_s else None
    before = [refs.pop(0) for _ in range(stacked)]
    total, dec = refs.pop(0), refs.pop(0)
    n, width = lat_t.shape[0], ex.shape[1]
    chunk = chunk_at(here, distance, weights.shape[1] // (2 * width))
    at_x, at_y = column(chunk, here[1], width), column(chunk, 1 - here[1], width)
    x, y = ex[...], ey[...]
    term = nt(x, weights[:, at_x]) + nt(y, weights[:, at_y])
    total[...] = term + total_in[...] if carried else term
    dec[:n, :] = jnp.dot(lat_t[...], x, preferred_element_type=F32).astype(BF16)
    dec[n:, :] = jnp.dot(lat_t[...], y, preferred_element_type=F32).astype(BF16)
    if sibling:
        total_s, dec_s = refs
        term = nt(x, weights_s[:, at_x]) + nt(y, weights_s[:, at_y])
        total_s[...] = term + total_s_in[...] if carried_s else term
        if stacked:
            for i, ref in enumerate(before):
                dec_s[i] = ref[...]
            dec_s = dec_s.at[stacked]
        dec_s[:n, :] = jnp.dot(lat_s[...], x, preferred_element_type=F32).astype(BF16)
        dec_s[n:, :] = jnp.dot(lat_s[...], y, preferred_element_type=F32).astype(BF16)


def cost(us):
    return pl.CostEstimate(flops=int(us * 1e9), bytes_accessed=1, transcendentals=0)


def kernel_call(body, args, out_shape, us=1):
    return pl.pallas_call(
        body,
        in_specs=[SMEM] + [VMEM] * (len(args) - 1),
        out_specs=jax.tree.map(lambda _: VMEM, out_shape),
        out_shape=out_shape,
        compiler_params=pltpu.CompilerParams(vmem_limit_bytes=VMEM_BYTES),
        cost_estimate=pl.CostEstimate(
            flops=int(us * 1e9),
            bytes_accessed=sum(x.size * x.dtype.itemsize for x in args + jax.tree.leaves(out_shape)),
            transcendentals=0,
        ),
    )(*args)


def step(here, distance, x, y, weights, lat_t, total=None, sibling=None, total_s=None, before=()):
    tokens, width = x.shape
    rows = weights.shape[0]
    grad = jax.ShapeDtypeStruct((tokens, rows), F32)
    block = (2 * rows, width)
    args = [here, x, y, weights, lat_t]
    out_shape = [grad, jax.ShapeDtypeStruct(block, BF16)]
    if sibling:
        args += list(sibling)
        out_shape += [
            grad,
            jax.ShapeDtypeStruct((len(before) + 1,) + block if before else block, BF16),
        ]
    args += [a for a in (total, total_s) if a is not None] + list(before)
    plan = (sibling is not None, total is not None, total_s is not None, len(before))
    return kernel_call(functools.partial(step_kernel, plan, distance), args, out_shape)


def place_kernel(own, here, ex, ey, lat_t, got, *refs):
    blocks, (keep, send) = refs[:own], refs[own:]
    n = lat_t.shape[0]
    half = keep.shape[0]
    nz = 2 * half

    def put(distance, top, bottom):
        chunk = chunk_at(here, distance, nz)
        mine = chunk // half == here[2]

        @pl.when(mine)
        def _():
            keep[chunk % half, :n, :] = top
            keep[chunk % half, n:, :] = bottom

        @pl.when(jnp.logical_not(mine))
        def _():
            send[chunk % half, :n, :] = top
            send[chunk % half, n:, :] = bottom

    put(
        half,
        jnp.dot(lat_t[...], ex[...], preferred_element_type=F32).astype(BF16),
        jnp.dot(lat_t[...], ey[...], preferred_element_type=F32).astype(BF16),
    )
    for k in range(own):
        put(k, blocks[k][:n, :], blocks[k][n:, :])
    for k in range(got.shape[0]):
        put(nz - k - 1, got[k, n:, :], got[k, :n, :])


def place(here, x, y, lat_t, got, blocks):
    part = jax.ShapeDtypeStruct((got.shape[0] + 1,) + blocks[0].shape, BF16)
    body = functools.partial(place_kernel, len(blocks))
    return kernel_call(body, [here, x, y, lat_t, got, *blocks], [part, part], 3)


def join_kernel(here, mine, other, out):
    n = mine.shape[1] // 2
    total = mine[0].astype(F32) + other[0].astype(F32)
    even = here[1] == 0
    out[:, :n] = jnp.where(even, total[:n], total[n:]).astype(BF16)
    out[:, n:] = jnp.where(even, total[n:], total[:n]).astype(BF16)


def join(here, mine, other):
    n, rows, width = other.shape
    return pl.pallas_call(
        join_kernel,
        grid_spec=pltpu.PrefetchScalarGridSpec(
            num_scalar_prefetch=1,
            grid=(n,),
            in_specs=[
                pl.BlockSpec((1, rows, width), lambda i, p: (i, 0, 0)),
                pl.BlockSpec((1, rows, width), lambda i, p: (i, 0, 0)),
            ],
            out_specs=pl.BlockSpec((rows // 2, 2 * width), lambda i, p: (0, i)),
        ),
        out_shape=jax.ShapeDtypeStruct((rows // 2, 2 * n * width), BF16),
        compiler_params=pltpu.CompilerParams(vmem_limit_bytes=VMEM_BYTES),
        cost_estimate=cost(4),
    )(here, mine, other)


def prologue_kernel(block, mask_ref, pre_ref, lat_ref, lat_t_ref):
    first = pl.program_id(0) * (pre_ref.shape[0] // block)
    for i in range(pre_ref.shape[0] // block):
        for j in range(pre_ref.shape[1] // block):
            at = (pl.ds(i * block, block), pl.ds(j * block, block))
            value = jnp.maximum(pre_ref[at].astype(F32), 0.0)
            value = jnp.where(mask_ref[j, first + i] > 0, value, 0.0)
            lat_ref[at] = value.astype(BF16)
            lat_t_ref[at[1], at[0]] = value.T.astype(BF16)


def prologue(block_mask, pre_acts):
    tokens, rows = pre_acts.shape
    block = tokens // block_mask.shape[0]
    n = 4
    return pl.pallas_call(
        functools.partial(prologue_kernel, block),
        grid_spec=pltpu.PrefetchScalarGridSpec(
            num_scalar_prefetch=1,
            grid=(n,),
            in_specs=[pl.BlockSpec((tokens // n, rows), lambda i, p: (i, 0))],
            out_specs=[
                pl.BlockSpec((tokens // n, rows), lambda i, p: (i, 0)),
                pl.BlockSpec((rows, tokens // n), lambda i, p: (0, i)),
            ],
        ),
        out_shape=[
            jax.ShapeDtypeStruct((tokens, rows), BF16),
            jax.ShapeDtypeStruct((rows, tokens), BF16),
        ],
        compiler_params=pltpu.CompilerParams(vmem_limit_bytes=VMEM_BYTES),
        cost_estimate=cost(4),
    )(block_mask.T, pre_acts)


def finish_kernel(here, ex, ey, weights, total, received, live, out):
    nz, width = weights.shape[1] // (2 * ex.shape[1]), ex.shape[1]
    chunk = chunk_at(here, nz // 2, nz)
    term = nt(ex[...], weights[:, column(chunk, here[1], width)])
    term += nt(ey[...], weights[:, column(chunk, 1 - here[1], width)])
    out[...] = jnp.where(live[...] > 0, term + total[...] + received[...], 0.0).astype(BF16)


def finish(here, x, y, weights, total, received, latents):
    out_shape = jax.ShapeDtypeStruct(latents.shape, BF16)
    return kernel_call(finish_kernel, [here, x, y, weights, total, received, latents], out_shape)


def sum_of(got):
    total = got[0].astype(F32)
    for i in range(1, got.shape[0]):
        total += got[i].astype(F32)
    return total.astype(BF16)


def sum_kernel(got, out):
    out[...] = sum_of(got)


def sum_part(got):
    return pl.pallas_call(
        sum_kernel,
        out_shape=jax.ShapeDtypeStruct(got.shape[1:], BF16),
        compiler_params=pltpu.CompilerParams(vmem_limit_bytes=VMEM_BYTES),
        cost_estimate=COST,
    )(got)


def spread_kernel(got, out):
    out[...] = jnp.broadcast_to(sum_of(got)[None], out.shape)


def exchange(terms, axis):
    n = lax.axis_size(axis)
    return lax.all_to_all(terms.reshape(n, terms.shape[0] // n, terms.shape[1]), axis, 0, 0)


def spread(got, axis):
    copies = pl.pallas_call(
        spread_kernel,
        out_shape=jax.ShapeDtypeStruct(got.shape, BF16),
        compiler_params=pltpu.CompilerParams(vmem_limit_bytes=VMEM_BYTES),
        cost_estimate=COST,
    )(got)
    return lax.all_to_all(copies, axis, 0, 0).reshape(-1, got.shape[2])


def input_kernel(delta, encoder, out):
    out[...] = nt(delta[...], encoder[...]).astype(BF16)


def input_part(delta, encoder):
    return pl.pallas_call(
        input_kernel,
        out_shape=jax.ShapeDtypeStruct((delta.shape[0], encoder.shape[0]), BF16),
        compiler_params=pltpu.CompilerParams(vmem_limit_bytes=VMEM_BYTES),
        cost_estimate=COST,
    )(delta, encoder)


def encoder_kernel(here, inputs, delta, keep, send):
    total = lax.dot_general(
        inputs[...], delta[...], (((0,), (0,)), ((), ())), preferred_element_type=F32
    )
    rows = keep.shape[0]
    low = here[2] == 0
    keep[...] = jnp.where(low, total[:rows], total[rows:])
    send[...] = jnp.where(low, total[rows:], total[:rows])


def encoder_part(here, inputs, delta):
    part = jax.ShapeDtypeStruct((inputs.shape[1] // 2, delta.shape[1]), F32)
    return kernel_call(encoder_kernel, [here, inputs, delta], [part, part], us=3)


def shards(errors, decoder, pre_acts, inputs, encoder, block_mask):
    n = lax.axis_size("lat")
    nz = n // 2
    me = lax.axis_index("lat")
    mine = lax.axis_index("tok")
    here = jnp.stack([me // 2, me % 2, mine]).astype(jnp.int32)
    swap = [(i, i ^ 1) for i in range(n)]
    ring = [(2 * k + c, 2 * ((k + 1 - 2 * c) % nz) + c) for k in range(nz) for c in range(2)]
    tok_swap = [(0, 1), (1, 0)]

    across = [(2 * k + c, 2 * ((k + 2 * c - 1) % nz) + 1 - c) for k in range(nz) for c in range(2)]

    own = errors[0]
    weights = decoder[0]
    x = lax.ppermute(own, "lat", ring)
    y = lax.ppermute(own, "lat", across)
    latents, lat_t = prologue(block_mask, pre_acts)
    _, _, lat_t = lax.optimization_barrier((x, y, lat_t))
    sibling = (lax.ppermute(weights, "lat", swap), lax.ppermute(lat_t, "lat", swap))
    last = nz // 2 - 1
    blocks, blocks_s, total, total_s = [], [], None, None
    for k in range(1, last + 1):
        if k == 2:
            x, near, total = lax.optimization_barrier((x, own, total))
            sib = lax.ppermute(near, "lat", swap)
            total, dec = step(here, 0, own, sib, weights, lat_t, total)
            blocks.insert(0, dec)
        elif k > 2:
            x, total = lax.optimization_barrier((x, total))
        nx = lax.ppermute(x, "lat", ring)
        ny = lax.ppermute(y, "lat", ring) if k < last else None
        before = blocks_s if k == last else []
        total, dec, total_s, dec_s = step(
            here, k, x, y, weights, lat_t, total, sibling, total_s, before
        )
        blocks.append(dec)
        blocks_s.append(dec_s)
        x, y = nx, ny
    x, total, total_s, dec_s = lax.optimization_barrier((x, total, total_s, dec_s))
    received = lax.ppermute(total_s, "lat", swap)
    y = lax.ppermute(x, "lat", swap)
    grad_part = finish(here, x, y, weights, total, received, latents)

    grad_part, dec_s = lax.optimization_barrier((grad_part, dec_s))
    dec_got = lax.ppermute(dec_s, "lat", swap)
    terms = exchange(grad_part, "tgt")
    keep, send = place(here, x, y, lat_t, dec_got, blocks)
    terms, send = lax.optimization_barrier((terms, send))
    other = lax.ppermute(send, "tok", tok_swap)
    delta = spread(terms, "tgt")

    terms = exchange(input_part(delta, encoder), "lat")
    enc_keep, enc_send = encoder_part(here, inputs, delta)
    enc_other = lax.ppermute(enc_send, "tok", tok_swap)
    dec_grad = join(here, keep, other)[None]
    enc_grad = enc_keep + enc_other
    terms, dec_grad, enc_grad = lax.optimization_barrier((terms, dec_grad, enc_grad))
    input_grad = lax.all_gather(sum_part(terms), "lat", axis=0, tiled=True)
    return (dec_grad, enc_grad, input_grad)


def solution(mesh):
    in_specs = (
        P("tgt", "tok", "lat"),
        P("tgt", "lat", None),
        P("tok", "lat"),
        P("tok", "tgt"),
        P("tgt", "lat"),
        P("tok", "lat"),
    )
    out_specs = (P("tgt", "lat", "tok"), P(("tgt", "tok"), "lat"), P("tok", "tgt"))
    return jax.shard_map(shards, mesh=mesh, in_specs=in_specs, out_specs=out_specs, check_vma=False)
```

```python
import functools

import jax
import jax.numpy as jnp
from jax import lax
from jax.experimental import pallas as pl
from jax.experimental.pallas import tpu as pltpu
from jax.sharding import PartitionSpec as P

F32 = jnp.float32
BF16 = jnp.bfloat16
VMEM_BYTES = 20 * 1024 * 1024
COST = pl.CostEstimate(flops=1, bytes_accessed=1, transcendentals=0)
SMEM = pl.BlockSpec(memory_space=pltpu.SMEM)
VMEM = pl.BlockSpec(memory_space=pltpu.VMEM)


def nt(a, b):
    return lax.dot_general(a, b, (((1,), (1,)), ((), ())), preferred_element_type=F32)


def chunk_at(here, distance, nz):
    return lax.rem(here[0] + (2 * here[1] - 1) * distance + nz, nz)


def column(chunk, core, width):
    return pl.ds(pl.multiple_of((2 * chunk + core) * width, width), width)


def step_kernel(plan, distance, here, *refs):
    sibling, carried, carried_s, stacked = plan
    refs = list(refs)
    ex, ey, weights, lat_t = (refs.pop(0) for _ in range(4))
    if sibling:
        weights_s, lat_s = refs.pop(0), refs.pop(0)
    total_in = refs.pop(0) if carried else None
    total_s_in = refs.pop(0) if carried_s else None
    before = [refs.pop(0) for _ in range(stacked)]
    total, dec = refs.pop(0), refs.pop(0)
    n, width = lat_t.shape[0], ex.shape[1]
    chunk = chunk_at(here, distance, weights.shape[1] // (2 * width))
    at_x, at_y = column(chunk, here[1], width), column(chunk, 1 - here[1], width)
    x, y = ex[...], ey[...]
    term = nt(x, weights[:, at_x]) + nt(y, weights[:, at_y])
    total[...] = term + total_in[...] if carried else term
    dec[:n, :] = jnp.dot(lat_t[...], x, preferred_element_type=F32).astype(BF16)
    dec[n:, :] = jnp.dot(lat_t[...], y, preferred_element_type=F32).astype(BF16)
    if sibling:
        total_s, dec_s = refs
        term = nt(x, weights_s[:, at_x]) + nt(y, weights_s[:, at_y])
        total_s[...] = term + total_s_in[...] if carried_s else term
        if stacked:
            for i, ref in enumerate(before):
                dec_s[i] = ref[...]
            dec_s = dec_s.at[stacked]
        dec_s[:n, :] = jnp.dot(lat_s[...], x, preferred_element_type=F32).astype(BF16)
        dec_s[n:, :] = jnp.dot(lat_s[...], y, preferred_element_type=F32).astype(BF16)


def cost(us):
    return pl.CostEstimate(flops=int(us * 1e9), bytes_accessed=1, transcendentals=0)


def kernel_call(body, args, out_shape, us=1):
    return pl.pallas_call(
        body,
        in_specs=[SMEM] + [VMEM] * (len(args) - 1),
        out_specs=jax.tree.map(lambda _: VMEM, out_shape),
        out_shape=out_shape,
        compiler_params=pltpu.CompilerParams(vmem_limit_bytes=VMEM_BYTES),
        cost_estimate=pl.CostEstimate(
            flops=int(us * 1e9),
            bytes_accessed=sum(x.size * x.dtype.itemsize for x in args + jax.tree.leaves(out_shape)),
            transcendentals=0,
        ),
    )(*args)


def step(here, distance, x, y, weights, lat_t, total=None, sibling=None, total_s=None, before=()):
    tokens, width = x.shape
    rows = weights.shape[0]
    grad = jax.ShapeDtypeStruct((tokens, rows), F32)
    block = (2 * rows, width)
    args = [here, x, y, weights, lat_t]
    out_shape = [grad, jax.ShapeDtypeStruct(block, BF16)]
    if sibling:
        args += list(sibling)
        out_shape += [
            grad,
            jax.ShapeDtypeStruct((len(before) + 1,) + block if before else block, BF16),
        ]
    args += [a for a in (total, total_s) if a is not None] + list(before)
    plan = (sibling is not None, total is not None, total_s is not None, len(before))
    return kernel_call(functools.partial(step_kernel, plan, distance), args, out_shape)


def place_kernel(own, here, ex, ey, lat_t, got, *refs):
    blocks, (keep, send) = refs[:own], refs[own:]
    n = lat_t.shape[0]
    half = keep.shape[0]
    nz = 2 * half

    def put(distance, top, bottom):
        chunk = chunk_at(here, distance, nz)
        mine = chunk // half == here[2]

        @pl.when(mine)
        def _():
            keep[chunk % half, :n, :] = top
            keep[chunk % half, n:, :] = bottom

        @pl.when(jnp.logical_not(mine))
        def _():
            send[chunk % half, :n, :] = top
            send[chunk % half, n:, :] = bottom

    put(
        half,
        jnp.dot(lat_t[...], ex[...], preferred_element_type=F32).astype(BF16),
        jnp.dot(lat_t[...], ey[...], preferred_element_type=F32).astype(BF16),
    )
    for k in range(own):
        put(k, blocks[k][:n, :], blocks[k][n:, :])
    for k in range(got.shape[0]):
        put(nz - k - 1, got[k, n:, :], got[k, :n, :])


def place(here, x, y, lat_t, got, blocks):
    part = jax.ShapeDtypeStruct((got.shape[0] + 1,) + blocks[0].shape, BF16)
    body = functools.partial(place_kernel, len(blocks))
    return kernel_call(body, [here, x, y, lat_t, got, *blocks], [part, part], 3)


def join_kernel(here, mine, other, out):
    n = mine.shape[1] // 2
    total = mine[0].astype(F32) + other[0].astype(F32)
    even = here[1] == 0
    out[:, :n] = jnp.where(even, total[:n], total[n:]).astype(BF16)
    out[:, n:] = jnp.where(even, total[n:], total[:n]).astype(BF16)


def join(here, mine, other):
    n, rows, width = other.shape
    return pl.pallas_call(
        join_kernel,
        grid_spec=pltpu.PrefetchScalarGridSpec(
            num_scalar_prefetch=1,
            grid=(n,),
            in_specs=[
                pl.BlockSpec((1, rows, width), lambda i, p: (i, 0, 0)),
                pl.BlockSpec((1, rows, width), lambda i, p: (i, 0, 0)),
            ],
            out_specs=pl.BlockSpec((rows // 2, 2 * width), lambda i, p: (0, i)),
        ),
        out_shape=jax.ShapeDtypeStruct((rows // 2, 2 * n * width), BF16),
        compiler_params=pltpu.CompilerParams(vmem_limit_bytes=VMEM_BYTES),
        cost_estimate=cost(4),
    )(here, mine, other)


def prologue_kernel(block, mask_ref, pre_ref, lat_ref, lat_t_ref):
    first = pl.program_id(0) * (pre_ref.shape[0] // block)
    for i in range(pre_ref.shape[0] // block):
        for j in range(pre_ref.shape[1] // block):
            at = (pl.ds(i * block, block), pl.ds(j * block, block))
            value = jnp.maximum(pre_ref[at].astype(F32), 0.0)
            value = jnp.where(mask_ref[j, first + i] > 0, value, 0.0)
            lat_ref[at] = value.astype(BF16)
            lat_t_ref[at[1], at[0]] = value.T.astype(BF16)


def prologue(block_mask, pre_acts):
    tokens, rows = pre_acts.shape
    block = tokens // block_mask.shape[0]
    n = 4
    return pl.pallas_call(
        functools.partial(prologue_kernel, block),
        grid_spec=pltpu.PrefetchScalarGridSpec(
            num_scalar_prefetch=1,
            grid=(n,),
            in_specs=[pl.BlockSpec((tokens // n, rows), lambda i, p: (i, 0))],
            out_specs=[
                pl.BlockSpec((tokens // n, rows), lambda i, p: (i, 0)),
                pl.BlockSpec((rows, tokens // n), lambda i, p: (0, i)),
            ],
        ),
        out_shape=[
            jax.ShapeDtypeStruct((tokens, rows), BF16),
            jax.ShapeDtypeStruct((rows, tokens), BF16),
        ],
        compiler_params=pltpu.CompilerParams(vmem_limit_bytes=VMEM_BYTES),
        cost_estimate=cost(4),
    )(block_mask.T, pre_acts)


def finish_kernel(here, ex, ey, weights, total, received, live, out):
    nz, width = weights.shape[1] // (2 * ex.shape[1]), ex.shape[1]
    chunk = chunk_at(here, nz // 2, nz)
    term = nt(ex[...], weights[:, column(chunk, here[1], width)])
    term += nt(ey[...], weights[:, column(chunk, 1 - here[1], width)])
    out[...] = jnp.where(live[...] > 0, term + total[...] + received[...], 0.0).astype(BF16)


def finish(here, x, y, weights, total, received, latents):
    out_shape = jax.ShapeDtypeStruct(latents.shape, BF16)
    return kernel_call(finish_kernel, [here, x, y, weights, total, received, latents], out_shape)


def sum_of(got):
    total = got[0].astype(F32)
    for i in range(1, got.shape[0]):
        total += got[i].astype(F32)
    return total.astype(BF16)


def sum_kernel(got, out):
    out[...] = sum_of(got)


def sum_part(got):
    return pl.pallas_call(
        sum_kernel,
        out_shape=jax.ShapeDtypeStruct(got.shape[1:], BF16),
        compiler_params=pltpu.CompilerParams(vmem_limit_bytes=VMEM_BYTES),
        cost_estimate=COST,
    )(got)


def spread_kernel(got, out):
    out[...] = jnp.broadcast_to(sum_of(got)[None], out.shape)


def exchange(terms, axis):
    n = lax.axis_size(axis)
    return lax.all_to_all(terms.reshape(n, terms.shape[0] // n, terms.shape[1]), axis, 0, 0)


def spread(got, axis):
    copies = pl.pallas_call(
        spread_kernel,
        out_shape=jax.ShapeDtypeStruct(got.shape, BF16),
        compiler_params=pltpu.CompilerParams(vmem_limit_bytes=VMEM_BYTES),
        cost_estimate=COST,
    )(got)
    return lax.all_to_all(copies, axis, 0, 0).reshape(-1, got.shape[2])


def input_kernel(delta, encoder, out):
    out[...] = nt(delta[...], encoder[...]).astype(BF16)


def input_part(delta, encoder):
    return pl.pallas_call(
        input_kernel,
        out_shape=jax.ShapeDtypeStruct((delta.shape[0], encoder.shape[0]), BF16),
        compiler_params=pltpu.CompilerParams(vmem_limit_bytes=VMEM_BYTES),
        cost_estimate=COST,
    )(delta, encoder)


def encoder_kernel(here, inputs, delta, keep, send):
    total = lax.dot_general(
        inputs[...], delta[...], (((0,), (0,)), ((), ())), preferred_element_type=F32
    )
    rows = keep.shape[0]
    low = here[2] == 0
    keep[...] = jnp.where(low, total[:rows], total[rows:])
    send[...] = jnp.where(low, total[rows:], total[:rows])


def encoder_part(here, inputs, delta):
    part = jax.ShapeDtypeStruct((inputs.shape[1] // 2, delta.shape[1]), F32)
    return kernel_call(encoder_kernel, [here, inputs, delta], [part, part], us=3)


def shards(errors, decoder, pre_acts, inputs, encoder, block_mask):
    n = lax.axis_size("lat")
    nz = n // 2
    me = lax.axis_index("lat")
    mine = lax.axis_index("tok")
    here = jnp.stack([me // 2, me % 2, mine]).astype(jnp.int32)
    swap = [(i, i ^ 1) for i in range(n)]
    ring = [(2 * k + c, 2 * ((k + 1 - 2 * c) % nz) + c) for k in range(nz) for c in range(2)]
    tok_swap = [(0, 1), (1, 0)]

    across = [(2 * k + c, 2 * ((k + 2 * c - 1) % nz) + 1 - c) for k in range(nz) for c in range(2)]

    own = errors[0]
    weights = decoder[0]
    latents, lat_t = prologue(block_mask, pre_acts)
    sibling = (lax.ppermute(weights, "lat", swap), lax.ppermute(lat_t, "lat", swap))
    y = lax.ppermute(own, "lat", across)
    x = lax.ppermute(own, "lat", ring)
    x, sibling = lax.optimization_barrier((x, sibling))
    last = nz // 2 - 1
    blocks, blocks_s, total, total_s = [], [], None, None
    for k in range(1, last + 1):
        if k == 2:
            x, near, total = lax.optimization_barrier((x, own, total))
            sib = lax.ppermute(near, "lat", swap)
        elif k > 2:
            x, total = lax.optimization_barrier((x, total))
        nx = lax.ppermute(x, "lat", ring)
        ny = lax.ppermute(y, "lat", ring) if k < last else None
        if k == last:
            total, dec = step(here, 0, own, sib, weights, lat_t, total)
            blocks.insert(0, dec)
        before = blocks_s if k == last else []
        total, dec, total_s, dec_s = step(
            here, k, x, y, weights, lat_t, total, sibling, total_s, before
        )
        blocks.append(dec)
        blocks_s.append(dec_s)
        x, y = nx, ny
    x, total, total_s, dec_s = lax.optimization_barrier((x, total, total_s, dec_s))
    received = lax.ppermute(total_s, "lat", swap)
    y = lax.ppermute(x, "lat", swap)
    grad_part = finish(here, x, y, weights, total, received, latents)

    grad_part, dec_s = lax.optimization_barrier((grad_part, dec_s))
    dec_got = lax.ppermute(dec_s, "lat", swap)
    terms = exchange(grad_part, "tgt")
    keep, send = place(here, x, y, lat_t, dec_got, blocks)
    terms, send = lax.optimization_barrier((terms, send))
    other = lax.ppermute(send, "tok", tok_swap)
    delta = spread(terms, "tgt")

    terms = exchange(input_part(delta, encoder), "lat")
    enc_keep, enc_send = encoder_part(here, inputs, delta)
    enc_other = lax.ppermute(enc_send, "tok", tok_swap)
    dec_grad = join(here, keep, other)[None]
    enc_grad = enc_keep + enc_other
    terms, dec_grad, enc_grad = lax.optimization_barrier((terms, dec_grad, enc_grad))
    input_grad = lax.all_gather(sum_part(terms), "lat", axis=0, tiled=True)
    return (dec_grad, enc_grad, input_grad)


def solution(mesh):
    in_specs = (
        P("tgt", "tok", "lat"),
        P("tgt", "lat", None),
        P("tok", "lat"),
        P("tok", "tgt"),
        P("tgt", "lat"),
        P("tok", "lat"),
    )
    out_specs = (P("tgt", "lat", "tok"), P(("tgt", "tok"), "lat"), P("tok", "tgt"))
    return jax.shard_map(shards, mesh=mesh, in_specs=in_specs, out_specs=out_specs, check_vma=False)
```

```python
import functools

import jax
import jax.numpy as jnp
from jax import lax
from jax.experimental import pallas as pl
from jax.experimental.pallas import tpu as pltpu
from jax.sharding import PartitionSpec as P

F32 = jnp.float32
BF16 = jnp.bfloat16
VMEM_BYTES = 20 * 1024 * 1024
COST = pl.CostEstimate(flops=1, bytes_accessed=1, transcendentals=0)
SMEM = pl.BlockSpec(memory_space=pltpu.SMEM)
VMEM = pl.BlockSpec(memory_space=pltpu.VMEM)


def nt(a, b):
    return lax.dot_general(a, b, (((1,), (1,)), ((), ())), preferred_element_type=F32)


def chunk_at(here, distance, nz):
    return lax.rem(here[0] + (2 * here[1] - 1) * distance + nz, nz)


def column(chunk, core, width):
    return pl.ds(pl.multiple_of((2 * chunk + core) * width, width), width)


def step_kernel(plan, distance, here, *refs):
    sibling, carried, carried_s, stacked = plan
    refs = list(refs)
    ex, ey, weights, lat_t = (refs.pop(0) for _ in range(4))
    if sibling:
        weights_s, lat_s = refs.pop(0), refs.pop(0)
    total_in = refs.pop(0) if carried else None
    total_s_in = refs.pop(0) if carried_s else None
    before = [refs.pop(0) for _ in range(stacked)]
    total, dec = refs.pop(0), refs.pop(0)
    n, width = lat_t.shape[0], ex.shape[1]
    chunk = chunk_at(here, distance, weights.shape[1] // (2 * width))
    at_x, at_y = column(chunk, here[1], width), column(chunk, 1 - here[1], width)
    x, y = ex[...], ey[...]
    term = nt(x, weights[:, at_x]) + nt(y, weights[:, at_y])
    total[...] = term + total_in[...] if carried else term
    dec[:n, :] = jnp.dot(lat_t[...], x, preferred_element_type=F32).astype(BF16)
    dec[n:, :] = jnp.dot(lat_t[...], y, preferred_element_type=F32).astype(BF16)
    if sibling:
        total_s, dec_s = refs
        term = nt(x, weights_s[:, at_x]) + nt(y, weights_s[:, at_y])
        total_s[...] = term + total_s_in[...] if carried_s else term
        if stacked:
            for i, ref in enumerate(before):
                dec_s[i] = ref[...]
            dec_s = dec_s.at[stacked]
        dec_s[:n, :] = jnp.dot(lat_s[...], x, preferred_element_type=F32).astype(BF16)
        dec_s[n:, :] = jnp.dot(lat_s[...], y, preferred_element_type=F32).astype(BF16)


def cost(us):
    return pl.CostEstimate(flops=int(us * 1e9), bytes_accessed=1, transcendentals=0)


def kernel_call(body, args, out_shape, us=1):
    return pl.pallas_call(
        body,
        in_specs=[SMEM] + [VMEM] * (len(args) - 1),
        out_specs=jax.tree.map(lambda _: VMEM, out_shape),
        out_shape=out_shape,
        compiler_params=pltpu.CompilerParams(vmem_limit_bytes=VMEM_BYTES),
        cost_estimate=pl.CostEstimate(
            flops=int(us * 1e9),
            bytes_accessed=sum(x.size * x.dtype.itemsize for x in args + jax.tree.leaves(out_shape)),
            transcendentals=0,
        ),
    )(*args)


def step(here, distance, x, y, weights, lat_t, total=None, sibling=None, total_s=None, before=()):
    tokens, width = x.shape
    rows = weights.shape[0]
    grad = jax.ShapeDtypeStruct((tokens, rows), F32)
    block = (2 * rows, width)
    args = [here, x, y, weights, lat_t]
    out_shape = [grad, jax.ShapeDtypeStruct(block, BF16)]
    if sibling:
        args += list(sibling)
        out_shape += [
            grad,
            jax.ShapeDtypeStruct((len(before) + 1,) + block if before else block, BF16),
        ]
    args += [a for a in (total, total_s) if a is not None] + list(before)
    plan = (sibling is not None, total is not None, total_s is not None, len(before))
    return kernel_call(functools.partial(step_kernel, plan, distance), args, out_shape)


def place_kernel(own, here, ex, ey, lat_t, got, *refs):
    blocks, (keep, send) = refs[:own], refs[own:]
    n = lat_t.shape[0]
    half = keep.shape[0]
    nz = 2 * half

    def put(distance, top, bottom):
        chunk = chunk_at(here, distance, nz)
        mine = chunk // half == here[2]

        @pl.when(mine)
        def _():
            keep[chunk % half, :n, :] = top
            keep[chunk % half, n:, :] = bottom

        @pl.when(jnp.logical_not(mine))
        def _():
            send[chunk % half, :n, :] = top
            send[chunk % half, n:, :] = bottom

    put(
        half,
        jnp.dot(lat_t[...], ex[...], preferred_element_type=F32).astype(BF16),
        jnp.dot(lat_t[...], ey[...], preferred_element_type=F32).astype(BF16),
    )
    for k in range(own):
        put(k, blocks[k][:n, :], blocks[k][n:, :])
    for k in range(got.shape[0]):
        put(nz - k - 1, got[k, n:, :], got[k, :n, :])


def place(here, x, y, lat_t, got, blocks):
    part = jax.ShapeDtypeStruct((got.shape[0] + 1,) + blocks[0].shape, BF16)
    body = functools.partial(place_kernel, len(blocks))
    return kernel_call(body, [here, x, y, lat_t, got, *blocks], [part, part], 3)


def join_kernel(here, mine, other, out):
    n, rows, width = mine.shape
    even = here[1] == 0
    for i in range(n):
        total = mine[i].astype(F32) + other[i].astype(F32)
        top, bottom = total[: rows // 2], total[rows // 2 :]
        out[:, 2 * i * width : (2 * i + 1) * width] = jnp.where(even, top, bottom).astype(BF16)
        out[:, (2 * i + 1) * width : (2 * i + 2) * width] = jnp.where(even, bottom, top).astype(BF16)


def join(here, mine, other):
    n, rows, width = mine.shape
    out_shape = jax.ShapeDtypeStruct((rows // 2, 2 * n * width), BF16)
    return kernel_call(join_kernel, [here, mine, other], out_shape, 2)


def prologue_kernel(block, mask_ref, pre_ref, lat_ref, lat_t_ref):
    first = pl.program_id(0) * (pre_ref.shape[0] // block)
    for i in range(pre_ref.shape[0] // block):
        for j in range(pre_ref.shape[1] // block):
            at = (pl.ds(i * block, block), pl.ds(j * block, block))
            value = jnp.maximum(pre_ref[at].astype(F32), 0.0)
            value = jnp.where(mask_ref[j, first + i] > 0, value, 0.0)
            lat_ref[at] = value.astype(BF16)
            lat_t_ref[at[1], at[0]] = value.T.astype(BF16)


def prologue(block_mask, pre_acts):
    tokens, rows = pre_acts.shape
    block = tokens // block_mask.shape[0]
    n = 4
    return pl.pallas_call(
        functools.partial(prologue_kernel, block),
        grid_spec=pltpu.PrefetchScalarGridSpec(
            num_scalar_prefetch=1,
            grid=(n,),
            in_specs=[pl.BlockSpec((tokens // n, rows), lambda i, p: (i, 0))],
            out_specs=[
                pl.BlockSpec((tokens // n, rows), lambda i, p: (i, 0)),
                pl.BlockSpec((rows, tokens // n), lambda i, p: (0, i)),
            ],
        ),
        out_shape=[
            jax.ShapeDtypeStruct((tokens, rows), BF16),
            jax.ShapeDtypeStruct((rows, tokens), BF16),
        ],
        compiler_params=pltpu.CompilerParams(vmem_limit_bytes=VMEM_BYTES),
        cost_estimate=cost(4),
    )(block_mask.T, pre_acts)


def finish_kernel(here, ex, ey, weights, total, received, live, out):
    nz, width = weights.shape[1] // (2 * ex.shape[1]), ex.shape[1]
    chunk = chunk_at(here, nz // 2, nz)
    term = nt(ex[...], weights[:, column(chunk, here[1], width)])
    term += nt(ey[...], weights[:, column(chunk, 1 - here[1], width)])
    out[...] = jnp.where(live[...] > 0, term + total[...] + received[...], 0.0).astype(BF16)


def finish(here, x, y, weights, total, received, latents):
    out_shape = jax.ShapeDtypeStruct(latents.shape, BF16)
    return kernel_call(finish_kernel, [here, x, y, weights, total, received, latents], out_shape)


def sum_of(got):
    total = got[0].astype(F32)
    for i in range(1, got.shape[0]):
        total += got[i].astype(F32)
    return total.astype(BF16)


def sum_kernel(got, out):
    out[...] = sum_of(got)


def sum_part(got):
    return pl.pallas_call(
        sum_kernel,
        out_shape=jax.ShapeDtypeStruct(got.shape[1:], BF16),
        compiler_params=pltpu.CompilerParams(vmem_limit_bytes=VMEM_BYTES),
        cost_estimate=COST,
    )(got)


def spread_kernel(got, out):
    out[...] = jnp.broadcast_to(sum_of(got)[None], out.shape)


def exchange(terms, axis):
    n = lax.axis_size(axis)
    return lax.all_to_all(terms.reshape(n, terms.shape[0] // n, terms.shape[1]), axis, 0, 0)


def spread(got, axis):
    copies = pl.pallas_call(
        spread_kernel,
        out_shape=jax.ShapeDtypeStruct(got.shape, BF16),
        compiler_params=pltpu.CompilerParams(vmem_limit_bytes=VMEM_BYTES),
        cost_estimate=COST,
    )(got)
    return lax.all_to_all(copies, axis, 0, 0).reshape(-1, got.shape[2])


def input_kernel(delta, encoder, out):
    out[...] = nt(delta[...], encoder[...]).astype(BF16)


def input_part(delta, encoder):
    return pl.pallas_call(
        input_kernel,
        out_shape=jax.ShapeDtypeStruct((delta.shape[0], encoder.shape[0]), BF16),
        compiler_params=pltpu.CompilerParams(vmem_limit_bytes=VMEM_BYTES),
        cost_estimate=COST,
    )(delta, encoder)


def encoder_kernel(here, inputs, delta, keep, send):
    total = lax.dot_general(
        inputs[...], delta[...], (((0,), (0,)), ((), ())), preferred_element_type=F32
    )
    rows = keep.shape[0]
    low = here[2] == 0
    keep[...] = jnp.where(low, total[:rows], total[rows:])
    send[...] = jnp.where(low, total[rows:], total[:rows])


def encoder_part(here, inputs, delta):
    part = jax.ShapeDtypeStruct((inputs.shape[1] // 2, delta.shape[1]), F32)
    return kernel_call(encoder_kernel, [here, inputs, delta], [part, part], us=3)


def shards(errors, decoder, pre_acts, inputs, encoder, block_mask):
    n = lax.axis_size("lat")
    nz = n // 2
    me = lax.axis_index("lat")
    mine = lax.axis_index("tok")
    here = jnp.stack([me // 2, me % 2, mine]).astype(jnp.int32)
    swap = [(i, i ^ 1) for i in range(n)]
    ring = [(2 * k + c, 2 * ((k + 1 - 2 * c) % nz) + c) for k in range(nz) for c in range(2)]
    tok_swap = [(0, 1), (1, 0)]

    across = [(2 * k + c, 2 * ((k + 2 * c - 1) % nz) + 1 - c) for k in range(nz) for c in range(2)]

    own = errors[0]
    weights = decoder[0]
    latents, lat_t = prologue(block_mask, pre_acts)
    sibling = (lax.ppermute(weights, "lat", swap), lax.ppermute(lat_t, "lat", swap))
    y = lax.ppermute(own, "lat", across)
    x = lax.ppermute(own, "lat", ring)
    x, sibling = lax.optimization_barrier((x, sibling))
    last = nz // 2 - 1
    blocks, blocks_s, total, total_s = [], [], None, None
    for k in range(1, last + 1):
        if k == 2:
            x, near, total = lax.optimization_barrier((x, own, total))
            sib = lax.ppermute(near, "lat", swap)
        elif k > 2:
            x, total = lax.optimization_barrier((x, total))
        nx = lax.ppermute(x, "lat", ring)
        ny = lax.ppermute(y, "lat", ring) if k < last else None
        if k == last:
            total, dec = step(here, 0, own, sib, weights, lat_t, total)
            blocks.insert(0, dec)
        before = blocks_s if k == last else []
        total, dec, total_s, dec_s = step(
            here, k, x, y, weights, lat_t, total, sibling, total_s, before
        )
        blocks.append(dec)
        blocks_s.append(dec_s)
        x, y = nx, ny
    received = lax.ppermute(total_s, "lat", swap)
    x, total, dec_s = lax.optimization_barrier((x, total, dec_s))
    dec_got = lax.ppermute(dec_s, "lat", swap)
    y = lax.ppermute(x, "lat", swap)
    grad_part = finish(here, x, y, weights, total, received, latents)

    terms = exchange(grad_part, "tgt")
    keep, send = place(here, x, y, lat_t, dec_got, blocks)
    terms, send = lax.optimization_barrier((terms, send))
    other = lax.ppermute(send, "tok", tok_swap)
    delta = spread(terms, "tgt")

    terms = exchange(input_part(delta, encoder), "lat")
    enc_keep, enc_send = encoder_part(here, inputs, delta)
    enc_other = lax.ppermute(enc_send, "tok", tok_swap)
    dec_grad = join(here, keep, other)[None]
    enc_grad = enc_keep + enc_other
    terms, dec_grad = lax.optimization_barrier((terms, dec_grad))
    input_grad = lax.all_gather(sum_part(terms), "lat", axis=0, tiled=True)
    return (dec_grad, enc_grad, input_grad)


def solution(mesh):
    in_specs = (
        P("tgt", "tok", "lat"),
        P("tgt", "lat", None),
        P("tok", "lat"),
        P("tok", "tgt"),
        P("tgt", "lat"),
        P("tok", "lat"),
    )
    out_specs = (P("tgt", "lat", "tok"), P(("tgt", "tok"), "lat"), P("tok", "tgt"))
    return jax.shard_map(shards, mesh=mesh, in_specs=in_specs, out_specs=out_specs, check_vma=False)
```

```python
import functools

import jax
import jax.numpy as jnp
from jax import lax
from jax.experimental import pallas as pl
from jax.experimental.pallas import tpu as pltpu
from jax.sharding import PartitionSpec as P

F32 = jnp.float32
BF16 = jnp.bfloat16
VMEM_BYTES = 20 * 1024 * 1024
COST = pl.CostEstimate(flops=1, bytes_accessed=1, transcendentals=0)
SMEM = pl.BlockSpec(memory_space=pltpu.SMEM)
VMEM = pl.BlockSpec(memory_space=pltpu.VMEM)


def nt(a, b):
    return lax.dot_general(a, b, (((1,), (1,)), ((), ())), preferred_element_type=F32)


def chunk_at(here, distance, nz):
    return lax.rem(here[0] + (2 * here[1] - 1) * distance + nz, nz)


def column(chunk, core, width):
    return pl.ds(pl.multiple_of((2 * chunk + core) * width, width), width)


def step_kernel(plan, distance, here, *refs):
    sibling, carried, carried_s, stacked = plan
    refs = list(refs)
    ex, ey, weights, lat_t = (refs.pop(0) for _ in range(4))
    if sibling:
        weights_s, lat_s = refs.pop(0), refs.pop(0)
    total_in = refs.pop(0) if carried else None
    total_s_in = refs.pop(0) if carried_s else None
    before = [refs.pop(0) for _ in range(stacked)]
    total, dec = refs.pop(0), refs.pop(0)
    n, width = lat_t.shape[0], ex.shape[1]
    chunk = chunk_at(here, distance, weights.shape[1] // (2 * width))
    at_x, at_y = column(chunk, here[1], width), column(chunk, 1 - here[1], width)
    x, y = ex[...], ey[...]
    term = nt(x, weights[:, at_x]) + nt(y, weights[:, at_y])
    total[...] = term + total_in[...] if carried else term
    dec[:n, :] = jnp.dot(lat_t[...], x, preferred_element_type=F32).astype(BF16)
    dec[n:, :] = jnp.dot(lat_t[...], y, preferred_element_type=F32).astype(BF16)
    if sibling:
        total_s, dec_s = refs
        term = nt(x, weights_s[:, at_x]) + nt(y, weights_s[:, at_y])
        total_s[...] = term + total_s_in[...] if carried_s else term
        if stacked:
            for i, ref in enumerate(before):
                dec_s[i] = ref[...]
            dec_s = dec_s.at[stacked]
        dec_s[:n, :] = jnp.dot(lat_s[...], x, preferred_element_type=F32).astype(BF16)
        dec_s[n:, :] = jnp.dot(lat_s[...], y, preferred_element_type=F32).astype(BF16)


def cost(us):
    return pl.CostEstimate(flops=int(us * 1e9), bytes_accessed=1, transcendentals=0)


def kernel_call(body, args, out_shape, us=1):
    return pl.pallas_call(
        body,
        in_specs=[SMEM] + [VMEM] * (len(args) - 1),
        out_specs=jax.tree.map(lambda _: VMEM, out_shape),
        out_shape=out_shape,
        compiler_params=pltpu.CompilerParams(vmem_limit_bytes=VMEM_BYTES),
        cost_estimate=pl.CostEstimate(
            flops=int(us * 1e9),
            bytes_accessed=sum(x.size * x.dtype.itemsize for x in args + jax.tree.leaves(out_shape)),
            transcendentals=0,
        ),
    )(*args)


def step(here, distance, x, y, weights, lat_t, total=None, sibling=None, total_s=None, before=()):
    tokens, width = x.shape
    rows = weights.shape[0]
    grad = jax.ShapeDtypeStruct((tokens, rows), F32)
    block = (2 * rows, width)
    args = [here, x, y, weights, lat_t]
    out_shape = [grad, jax.ShapeDtypeStruct(block, BF16)]
    if sibling:
        args += list(sibling)
        out_shape += [
            grad,
            jax.ShapeDtypeStruct((len(before) + 1,) + block if before else block, BF16),
        ]
    args += [a for a in (total, total_s) if a is not None] + list(before)
    plan = (sibling is not None, total is not None, total_s is not None, len(before))
    return kernel_call(functools.partial(step_kernel, plan, distance), args, out_shape)


def place_kernel(own, here, ex, ey, lat_t, got, *refs):
    blocks, (keep, send) = refs[:own], refs[own:]
    n = lat_t.shape[0]
    half = keep.shape[0]
    nz = 2 * half

    def put(distance, top, bottom):
        chunk = chunk_at(here, distance, nz)
        mine = chunk // half == here[2]

        @pl.when(mine)
        def _():
            keep[chunk % half, :n, :] = top
            keep[chunk % half, n:, :] = bottom

        @pl.when(jnp.logical_not(mine))
        def _():
            send[chunk % half, :n, :] = top
            send[chunk % half, n:, :] = bottom

    put(
        half,
        jnp.dot(lat_t[...], ex[...], preferred_element_type=F32).astype(BF16),
        jnp.dot(lat_t[...], ey[...], preferred_element_type=F32).astype(BF16),
    )
    for k in range(own):
        put(k, blocks[k][:n, :], blocks[k][n:, :])
    for k in range(got.shape[0]):
        put(nz - k - 1, got[k, n:, :], got[k, :n, :])


def place(here, x, y, lat_t, got, blocks):
    part = jax.ShapeDtypeStruct((got.shape[0] + 1,) + blocks[0].shape, BF16)
    body = functools.partial(place_kernel, len(blocks))
    return kernel_call(body, [here, x, y, lat_t, got, *blocks], [part, part], 3)


def join_kernel(here, mine, other, out):
    n, rows, width = mine.shape
    even = here[1] == 0
    for i in range(n):
        total = mine[i].astype(F32) + other[i].astype(F32)
        top, bottom = total[: rows // 2], total[rows // 2 :]
        out[:, 2 * i * width : (2 * i + 1) * width] = jnp.where(even, top, bottom).astype(BF16)
        out[:, (2 * i + 1) * width : (2 * i + 2) * width] = jnp.where(even, bottom, top).astype(BF16)


def join(here, mine, other):
    n, rows, width = mine.shape
    out_shape = jax.ShapeDtypeStruct((rows // 2, 2 * n * width), BF16)
    return kernel_call(join_kernel, [here, mine, other], out_shape, 2)


def prologue_kernel(mask, pre_ref, lat_ref, lat_t_ref):
    block = pre_ref.shape[0] // mask.shape[1]
    for i in range(mask.shape[1]):
        for j in range(mask.shape[0]):
            at = (pl.ds(i * block, block), pl.ds(j * block, block))
            value = jnp.maximum(pre_ref[at].astype(F32), 0.0)
            value = jnp.where(mask[j, i] > 0, value, 0.0)
            lat_ref[at] = value.astype(BF16)
            lat_t_ref[at[1], at[0]] = value.T.astype(BF16)


def prologue(block_mask, pre_acts):
    out_shape = [
        jax.ShapeDtypeStruct(pre_acts.shape, BF16),
        jax.ShapeDtypeStruct(pre_acts.shape[::-1], BF16),
    ]
    return kernel_call(prologue_kernel, [block_mask.T, pre_acts], out_shape, 4)


def finish_kernel(here, ex, ey, weights, total, received, live, out):
    nz, width = weights.shape[1] // (2 * ex.shape[1]), ex.shape[1]
    chunk = chunk_at(here, nz // 2, nz)
    term = nt(ex[...], weights[:, column(chunk, here[1], width)])
    term += nt(ey[...], weights[:, column(chunk, 1 - here[1], width)])
    out[...] = jnp.where(live[...] > 0, term + total[...] + received[...], 0.0).astype(BF16)


def finish(here, x, y, weights, total, received, latents):
    out_shape = jax.ShapeDtypeStruct(latents.shape, BF16)
    return kernel_call(finish_kernel, [here, x, y, weights, total, received, latents], out_shape)


def sum_of(got):
    total = got[0].astype(F32)
    for i in range(1, got.shape[0]):
        total += got[i].astype(F32)
    return total.astype(BF16)


def sum_kernel(got, out):
    out[...] = sum_of(got)


def sum_part(got):
    return pl.pallas_call(
        sum_kernel,
        out_shape=jax.ShapeDtypeStruct(got.shape[1:], BF16),
        compiler_params=pltpu.CompilerParams(vmem_limit_bytes=VMEM_BYTES),
        cost_estimate=COST,
    )(got)


def spread_kernel(got, out):
    out[...] = jnp.broadcast_to(sum_of(got)[None], out.shape)


def exchange(terms, axis):
    n = lax.axis_size(axis)
    return lax.all_to_all(terms.reshape(n, terms.shape[0] // n, terms.shape[1]), axis, 0, 0)


def spread(got, axis):
    copies = pl.pallas_call(
        spread_kernel,
        out_shape=jax.ShapeDtypeStruct(got.shape, BF16),
        compiler_params=pltpu.CompilerParams(vmem_limit_bytes=VMEM_BYTES),
        cost_estimate=COST,
    )(got)
    return lax.all_to_all(copies, axis, 0, 0).reshape(-1, got.shape[2])


def input_kernel(delta, encoder, out):
    out[...] = nt(delta[...], encoder[...]).astype(BF16)


def input_part(delta, encoder):
    return pl.pallas_call(
        input_kernel,
        out_shape=jax.ShapeDtypeStruct((delta.shape[0], encoder.shape[0]), BF16),
        compiler_params=pltpu.CompilerParams(vmem_limit_bytes=VMEM_BYTES),
        cost_estimate=COST,
    )(delta, encoder)


def encoder_kernel(here, inputs, delta, keep, send):
    total = lax.dot_general(
        inputs[...], delta[...], (((0,), (0,)), ((), ())), preferred_element_type=F32
    )
    rows = keep.shape[0]
    low = here[2] == 0
    keep[...] = jnp.where(low, total[:rows], total[rows:])
    send[...] = jnp.where(low, total[rows:], total[:rows])


def encoder_part(here, inputs, delta):
    part = jax.ShapeDtypeStruct((inputs.shape[1] // 2, delta.shape[1]), F32)
    return kernel_call(encoder_kernel, [here, inputs, delta], [part, part], us=3)


def shards(errors, decoder, pre_acts, inputs, encoder, block_mask):
    n = lax.axis_size("lat")
    nz = n // 2
    me = lax.axis_index("lat")
    mine = lax.axis_index("tok")
    here = jnp.stack([me // 2, me % 2, mine]).astype(jnp.int32)
    swap = [(i, i ^ 1) for i in range(n)]
    ring = [(2 * k + c, 2 * ((k + 1 - 2 * c) % nz) + c) for k in range(nz) for c in range(2)]
    tok_swap = [(0, 1), (1, 0)]

    across = [(2 * k + c, 2 * ((k + 2 * c - 1) % nz) + 1 - c) for k in range(nz) for c in range(2)]

    own = errors[0]
    weights = decoder[0]
    latents, lat_t = prologue(block_mask, pre_acts)
    sibling = (lax.ppermute(weights, "lat", swap), lax.ppermute(lat_t, "lat", swap))
    y = lax.ppermute(own, "lat", across)
    x = lax.ppermute(own, "lat", ring)
    x, sibling = lax.optimization_barrier((x, sibling))
    last = nz // 2 - 1
    blocks, blocks_s, total, total_s = [], [], None, None
    for k in range(1, last + 1):
        if k == 2:
            x, near, total = lax.optimization_barrier((x, own, total))
            sib = lax.ppermute(near, "lat", swap)
        elif k > 2:
            x, total = lax.optimization_barrier((x, total))
        nx = lax.ppermute(x, "lat", ring)
        ny = lax.ppermute(y, "lat", ring) if k < last else None
        if k == last:
            total, dec = step(here, 0, own, sib, weights, lat_t, total)
            blocks.insert(0, dec)
        before = blocks_s if k == last else []
        total, dec, total_s, dec_s = step(
            here, k, x, y, weights, lat_t, total, sibling, total_s, before
        )
        blocks.append(dec)
        blocks_s.append(dec_s)
        x, y = nx, ny
    received = lax.ppermute(total_s, "lat", swap)
    x, total, dec_s = lax.optimization_barrier((x, total, dec_s))
    dec_got = lax.ppermute(dec_s, "lat", swap)
    y = lax.ppermute(x, "lat", swap)
    grad_part = finish(here, x, y, weights, total, received, latents)

    terms = exchange(grad_part, "tgt")
    keep, send = place(here, x, y, lat_t, dec_got, blocks)
    terms, send = lax.optimization_barrier((terms, send))
    other = lax.ppermute(send, "tok", tok_swap)
    delta = spread(terms, "tgt")

    terms = exchange(input_part(delta, encoder), "lat")
    enc_keep, enc_send = encoder_part(here, inputs, delta)
    enc_other = lax.ppermute(enc_send, "tok", tok_swap)
    dec_grad = join(here, keep, other)[None]
    enc_grad = enc_keep + enc_other
    terms, dec_grad = lax.optimization_barrier((terms, dec_grad))
    input_grad = lax.all_gather(sum_part(terms), "lat", axis=0, tiled=True)
    return (dec_grad, enc_grad, input_grad)


def solution(mesh):
    in_specs = (
        P("tgt", "tok", "lat"),
        P("tgt", "lat", None),
        P("tok", "lat"),
        P("tok", "tgt"),
        P("tgt", "lat"),
        P("tok", "lat"),
    )
    out_specs = (P("tgt", "lat", "tok"), P(("tgt", "tok"), "lat"), P("tok", "tgt"))
    return jax.shard_map(shards, mesh=mesh, in_specs=in_specs, out_specs=out_specs, check_vma=False)
```
